128 devices in a mesh: ctx: 16 (over y, z), vocab: 8 (over x, core).
Axes of the slice: x: 4, y: 4, z: 4, core: 2. Of those that a mesh axis runs over, the one named last changes fastest.
Arguments:
- hidden_policy: bfloat16 [2, 512, 5120], P(None, 'ctx', 'vocab'), may hold values from -360 to 360, as said below
- hidden_ref: bfloat16 [2, 512, 5120], P(None, 'ctx', 'vocab'), may hold values from -360 to 360, as said below
- head_policy: bfloat16 [5120, 147456], P(None, ('ctx', 'vocab')), may hold values from -0.078125 to 0.078125
- head_ref: bfloat16 [5120, 147456], P(None, ('ctx', 'vocab')), may hold values from -0.078125 to 0.078125
- token_ids: int32 [2, 512], P(None, 'ctx'), may hold values from 0 to 147455
- response_mask: int32 [2, 512], P(None, 'ctx'), may hold values 0 or 1
- done_flags: int32 [2, 512], P(None, 'ctx'), may hold values 0 or 1
- scores: float32 [2, 512], P(None, 'ctx'), may hold values from -6 to 6
- values: float32 [2, 512], P(None, 'ctx'), may hold values from -6 to 6
Outputs:
- rewards: float32 [2, 512], P(None, 'ctx')
- advantages: float32 [2, 512], P(None, 'ctx')
- returns: float32 [2, 512], P(None, 'ctx')
- logprobs: float32 [2, 512], P(None, 'ctx')
The draws below stay inside these ranges and needn't reach their ends.
Inputs may be any that keep to these rules, and one draw needn't show every extreme that they name: `hidden_policy`: each token's hidden state has a scale of its own. `hidden_ref`: each token's hidden state has a scale of its own.
All inputs are finite; a program needn't handle non-finite values. No bound on the sum of `response_mask` or of `done_flags` on one device may be relied on, other than what follows from the above.
Results may differ from the reference program's by a relative error of at most 0.0003.
Values may be sent and summed in bfloat16 or wider, within the bound.
No kernel may reach another device: no remote copies, remote signals or barrier semaphores. Data moves between devices by JAX's collectives and lax.ppermute only.
A program may use at most 128 MiB of HBM per device.

```python
import jax
import jax.numpy as jnp
from jax import lax

D = 5120
TOK_DEV = 32
SEQS = 2
L = 512
VOCAB = 147456
N_CTX = 16


def hidden_law(key):
    scale_key, value_key = jax.random.split(key)
    row_scale = jnp.exp(jax.random.uniform(scale_key, (SEQS, L, 1), jnp.float32, jnp.log(1.5), jnp.log(5.0)))
    values = jnp.clip(jax.random.normal(value_key, (SEQS, L, D), jnp.float32), -6.0, 6.0)
    return (row_scale * values).astype(jnp.bfloat16)


def draw_hidden_policy(key, part):
    key = jax.random.fold_in(key, 11)
    return hidden_law(key)


def draw_hidden_ref(key, part):
    key = jax.random.fold_in(key, 23)
    return hidden_law(key)


def touch_ends(array, key, smallest, high):
    index_at = [jax.random.randint(jax.random.fold_in(key, axis), (), 0, length) for axis, length in enumerate(array.shape)]
    main_axis = array.shape.index(max(array.shape))
    beside = index_at[:main_axis] + [(index_at[main_axis] + 1) % array.shape[main_axis]] + index_at[main_axis + 1:]
    return array.at[tuple(index_at)].set(smallest).at[tuple(beside)].set(high)


def shard_levels(stream_key, dims, cuts, low, high):
    level, own = 1.0, jax.random.fold_in(stream_key, 6)
    for position, blocks in cuts:
        draws = jnp.exp(jax.random.uniform(jax.random.fold_in(own, position), (blocks,), jnp.float32, low / len(cuts), high / len(cuts)))
        level = level * jnp.repeat(draws, dims[position] // blocks).reshape([-1 if axis == position else 1 for axis in range(len(dims))])
    return level


def gaussian(own_key, dims, scale, most, cuts=(), kind=jnp.bfloat16):
    values = jax.random.normal(own_key, dims, jnp.float32) * scale
    if len(cuts) > 0:
        values = shard_levels(own_key, dims, cuts, -0.22, 0.18) * values
    return jnp.clip(values, min=-most, max=most).astype(kind)


def setup_inputs(seed: int = 0) -> dict:
    arg_keys = jax.random.split(jax.random.key(seed), 10)
    hidden_policy = draw_hidden_policy(jax.random.fold_in(arg_keys[9], 71), 0)
    hidden_ref = draw_hidden_ref(jax.random.fold_in(arg_keys[9], 71), 0)
    head_policy = gaussian(arg_keys[2], (D, VOCAB), D ** -0.5, 0.078125, ((1, 128),))
    head_ref = gaussian(arg_keys[3], (D, VOCAB), D ** -0.5, 0.078125, ((1, 128),))
    token_ids = touch_ends(jax.random.randint(arg_keys[4], (SEQS, L), 0, VOCAB), jax.random.fold_in(arg_keys[4], 1), 0, VOCAB - 1).astype(jnp.int32)
    response_mask = touch_ends((jax.random.randint(arg_keys[5], (SEQS, L), 0, 4) < 3).astype(jnp.int32), jax.random.fold_in(arg_keys[5], 1), 0, 1)
    done_flags = touch_ends((jax.random.randint(arg_keys[6], (SEQS, L), 0, 64) < 1).astype(jnp.int32), jax.random.fold_in(arg_keys[6], 1), 0, 1)
    scores = gaussian(arg_keys[7], (SEQS, L), 1.0, 6.0, ((1, 16),), jnp.float32)
    values = gaussian(arg_keys[8], (SEQS, L), 1.0, 6.0, ((1, 16),), jnp.float32)
    return dict(hidden_policy=hidden_policy, hidden_ref=hidden_ref, head_policy=head_policy, head_ref=head_ref, token_ids=token_ids, response_mask=response_mask, done_flags=done_flags, scores=scores, values=values)


def block_stats(head_policy, head_ref, block):
    hid_p, hid_q, ids = block
    logits_p = jnp.dot(hid_p, head_policy, preferred_element_type=jnp.float32)
    logits_q = jnp.dot(hid_q, head_ref, preferred_element_type=jnp.float32)
    top_p = jnp.max(logits_p, axis=-1, keepdims=True)
    top_q = jnp.max(logits_q, axis=-1, keepdims=True)
    lz_p = top_p[:, 0] + jnp.log(jnp.sum(jnp.exp(logits_p - top_p), axis=-1))
    lz_q = top_q[:, 0] + jnp.log(jnp.sum(jnp.exp(logits_q - top_q), axis=-1))
    probs = jnp.exp(logits_p - lz_p[:, None])
    kl_val = jnp.sum(probs * (logits_p - logits_q), axis=-1) - lz_p + lz_q
    chosen = jnp.take_along_axis(logits_p, ids[:, None], axis=1)[:, 0] - lz_p
    return kl_val, chosen


def reference(hidden_policy, hidden_ref, head_policy, head_ref, token_ids, response_mask, done_flags, scores, values):
    rows = SEQS * TOK_DEV
    hp = hidden_policy.reshape(N_CTX, rows, D)
    hq = hidden_ref.reshape(N_CTX, rows, D)
    ids = token_ids.reshape(N_CTX, rows).astype(jnp.int32)

    def one_block(block):
        return block_stats(head_policy, head_ref, block)

    kl_val, chosen = lax.map(one_block, (hp, hq, ids))
    kl_val = kl_val.reshape(SEQS, L)
    logprobs = chosen.reshape(SEQS, L)
    mask = response_mask.astype(jnp.float32)
    done = done_flags.astype(jnp.float32)
    rewards = -0.05 * mask * kl_val + done * scores
    next_value = jnp.concatenate([values[:, 1:], jnp.zeros((SEQS, 1), jnp.float32)], axis=1)
    delta = rewards + (1.0 - done) * next_value - values
    coef = 0.998 * (1.0 - done)

    def step(carry, item):
        cval, dval = item
        new = dval + cval * carry
        return new, new

    _, gae = lax.scan(step, jnp.zeros((SEQS,), jnp.float32), (coef.T, delta.T), reverse=True)
    gae = gae.T
    return rewards, mask * gae, mask * (gae + values), logprobs
```

```python
import jax
import jax.numpy as jnp
import numpy as np
from jax import lax
from jax.experimental import pallas as pl
from jax.experimental.pallas import tpu as pltpu
from jax.sharding import Mesh, PartitionSpec as P

PLANE = ("y", "z")
CHIPS = ("y", "z", "x")


def swap_cores(value):
    return lax.ppermute(value, "core", [(0, 1), (1, 0)])


def stats_kernel(ids_ref, hidden_ref, head_p_ref, head_q_ref, out_ref, acc_p, acc_q):
    step = pl.program_id(0)
    depth = hidden_ref.shape[-1]
    rows, width = acc_p.shape
    chunk = 128

    def add(acc, head_ref, first):
        tokens = hidden_ref.shape[-2]
        for r in range(0, rows, chunk):
            part = hidden_ref[pl.ds(r // tokens, chunk // tokens)].reshape(chunk, depth)
            product = jnp.dot(part, head_ref[...], preferred_element_type=jnp.float32)

            @pl.when(first)
            def _():
                acc[pl.ds(r, chunk), :] = product

            @pl.when(jnp.logical_not(first))
            def _():
                acc[pl.ds(r, chunk), :] += product

    @pl.when(step < 4)
    def _():
        add(acc_p, head_p_ref, step == 0)

    @pl.when(step >= 4)
    def _():
        add(acc_q, head_q_ref, step == 4)

    @pl.when(step == 7)
    def _():
        for r in range(0, rows, chunk):
            logits_p = acc_p[pl.ds(r, chunk), :]
            logits_q = acc_q[pl.ds(r, chunk), :]
            top_p = jnp.max(logits_p, axis=-1, keepdims=True)
            expo = jnp.exp(logits_p - top_p)
            sum_p = jnp.sum(expo, axis=-1, keepdims=True)
            cross = jnp.sum(expo * (logits_p - logits_q), axis=-1, keepdims=True)
            top_q = jnp.max(logits_q, axis=-1, keepdims=True)
            sum_q = jnp.sum(jnp.exp(logits_q - top_q), axis=-1, keepdims=True)
            column = lax.broadcasted_iota(jnp.int32, (chunk, width), 1)
            chosen = jnp.sum(
                jnp.where(column == ids_ref[pl.ds(r, chunk), :], logits_p, 0.0), axis=-1, keepdims=True
            )
            lane = lax.broadcasted_iota(jnp.int32, (chunk, 128), 1)
            packed = jnp.where(lane == 0, top_p + jnp.log(sum_p), 0.0)
            packed = jnp.where(lane == 1, cross / sum_p, packed)
            packed = jnp.where(lane == 2, top_q + jnp.log(sum_q), packed)
            packed = jnp.where(lane == 3, chosen, packed)
            out_ref[:, pl.ds(r, chunk)] = packed.T[0:8, :]


def block_stats(ids, hidden, head_p, head_q):
    blocks, _, _, tokens, depth = hidden.shape
    rows = blocks * tokens
    width = head_p.shape[1]
    return pl.pallas_call(
        stats_kernel,
        grid=(8,),
        in_specs=[
            pl.BlockSpec((rows, 1), lambda s: (0, 0)),
            pl.BlockSpec((blocks, None, None, tokens, depth), lambda s: (0, s % 4, s // 4, 0, 0)),
            pl.BlockSpec((depth, width), lambda s: (jnp.minimum(s, 3), 0)),
            pl.BlockSpec((depth, width), lambda s: (jnp.maximum(s - 4, 0), 0)),
        ],
        out_specs=pl.BlockSpec((8, rows), lambda s: (0, 0)),
        out_shape=jax.ShapeDtypeStruct((8, rows), jnp.float32),
        scratch_shapes=[pltpu.VMEM((rows, width), jnp.float32)] * 2,
        compiler_params=pltpu.CompilerParams(vmem_limit_bytes=48 << 20),
        cost_estimate=pl.CostEstimate(
            flops=4 * rows * 4 * depth * width,
            bytes_accessed=2 * 4 * depth * (width + rows) * 2,
            transcendentals=2 * rows * width,
        ),
        name="block_stats",
    )(ids, hidden, head_p, head_q)


def chain_products(coef):
    count = coef.shape[1]
    t = lax.broadcasted_iota(jnp.int32, (1, count, count), 1)
    u = lax.broadcasted_iota(jnp.int32, (1, count, count), 2)
    before = jnp.concatenate([jnp.ones_like(coef[:, :1]), coef[:, :-1]], axis=1)
    factors = jnp.where(u > t, before[:, None, :], 1.0)
    shift = 1
    while shift < count:
        moved = jnp.pad(factors[:, :, :-shift], ((0, 0), (0, 0), (shift, 0)), constant_values=1.0)
        factors = factors * moved
        shift *= 2
    return jnp.where(u >= t, factors, 0.0)


def body(hidden_policy, hidden_ref, head_policy, head_ref, token_ids, response_mask, done_flags, scores, values):
    y, z, x, core = (lax.axis_index(a) for a in ("y", "z", "x", "core"))
    width = head_policy.shape[1]
    tok = token_ids.shape[1]
    ctx = y * 4 + z
    first = core == 0

    def mine(pair):
        return jnp.where(first, pair[0], pair[1])

    def other(pair):
        return jnp.where(first, pair[1], pair[0])

    both = jnp.stack([hidden_policy, hidden_ref], axis=1)
    kept, given = mine(both), other(both)
    got = swap_cores(given)
    halves = jnp.concatenate([jnp.where(first, kept, got), jnp.where(first, got, kept)], axis=-1)
    hidden = lax.all_gather(halves, CHIPS)
    hidden = hidden.reshape((16, 4) + halves.shape)

    other_p, other_q = swap_cores(head_policy), swap_cores(head_ref)

    mask = response_mask.astype(jnp.float32)
    done = done_flags.astype(jnp.float32)
    coef = 0.998 * (1.0 - done)
    products = chain_products(coef)
    decay = products[:, :, -1] * coef[:, -1:]
    shared = jnp.concatenate(
        [token_ids.astype(jnp.float32), decay[:, :1], values[:, :1], jnp.zeros((2, 30), jnp.float32)], axis=1
    )
    shared = lax.all_to_all(jnp.broadcast_to(shared.reshape(1, 128), (16, 128)), PLANE, 0, 0, tiled=True)
    shared = shared.reshape(16, 2, 64)
    ids = mine(jnp.moveaxis(shared[:, :, :tok], 1, 0)).reshape(16 * tok).astype(jnp.int32)
    place = lax.broadcasted_iota(jnp.int32, (1, 16), 1)
    head_decay = shared[:, :, tok].T
    first_value = shared[:, :, tok + 1].T
    following = jnp.sum(jnp.where(place == ctx + 1, first_value, 0.0), axis=1, keepdims=True)
    next_value = jnp.concatenate([values[:, 1:], following], axis=1)
    known = done * scores + (1.0 - done) * next_value - values
    later = chain_products(head_decay)
    weights = jnp.sum(
        jnp.where(lax.broadcasted_iota(jnp.int32, (1, 16, 1), 1) == ctx + 1, later, 0.0), axis=1
    )

    columns = (ctx * 8 + x * 2) * width
    parts = []
    for k, heads in ((core, (head_policy, head_ref)), (1 - core, (other_p, other_q))):
        local = (ids - (columns + k * width))[:, None]
        parts.append(block_stats(local, hidden, *heads)[:4])
    stats = jnp.stack(parts).reshape(2, 4, 16, tok).transpose(2, 1, 0, 3).reshape(16, 1, 8 * tok)
    stats = jnp.broadcast_to(stats, (16, 4, 8 * tok)).reshape(64, 8 * tok)
    stats = lax.all_to_all(stats, CHIPS, 0, 0, tiled=True)
    stats = stats.reshape(64, 4, 2, tok)
    lse_p, ratio, lse_q, chosen = (stats[:, i] for i in range(4))
    top_p = jnp.max(lse_p, axis=(0, 1))
    w_p = jnp.exp(lse_p - top_p)
    total = jnp.sum(w_p, axis=(0, 1))
    lz_p = top_p + jnp.log(total)
    top_q = jnp.max(lse_q, axis=(0, 1))
    lz_q = top_q + jnp.log(jnp.sum(jnp.exp(lse_q - top_q), axis=(0, 1)))
    kl_val = jnp.sum(w_p * ratio, axis=(0, 1)) / total - lz_p + lz_q
    logprobs = jnp.sum(chosen, axis=(0, 1)) - lz_p
    penalty = -0.05 * mine(mask) * kl_val
    rewards = penalty + mine(done * scores)
    delta = penalty + mine(known)
    local_gae = jnp.sum(mine(products) * delta[None, :], axis=1)
    heads = lax.all_to_all(jnp.broadcast_to(local_gae[:1], (16, 1)), PLANE, 0, 0, tiled=True)
    incoming = jnp.sum(mine(weights) * heads[:, 0])
    gae = local_gae + mine(decay) * incoming
    own = jnp.stack([rewards, mine(mask) * gae, mine(mask) * (gae + mine(values)), logprobs])
    theirs = swap_cores(own)
    return tuple(
        jnp.stack([jnp.where(first, own[i], theirs[i]), jnp.where(first, theirs[i], own[i])]) for i in range(4)
    )


def solution(mesh):
    fine = Mesh(np.asarray(mesh.devices).reshape(4, 4, 4, 2), ("y", "z", "x", "core"))
    vocab = ("x", "core")
    placed = (
        P(None, PLANE, vocab),
        P(None, PLANE, vocab),
        P(None, PLANE + vocab),
        P(None, PLANE + vocab),
        P(None, PLANE),
        P(None, PLANE),
        P(None, PLANE),
        P(None, PLANE),
        P(None, PLANE),
    )
    return jax.shard_map(
        body,
        mesh=fine,
        in_specs=placed,
        out_specs=(P(None, PLANE),) * 4,
        check_vma=False,
    )
```

```python
import functools

import jax
import jax.numpy as jnp
import numpy as np
from jax import lax
from jax.experimental import pallas as pl
from jax.experimental.pallas import tpu as pltpu
from jax.sharding import Mesh, PartitionSpec as P


PLANE = ("y", "z")
VOCAB = ("x", "core")
ALL = PLANE + VOCAB
SHARED = 16
HALF = (64 - SHARED) // 2
STARTS = (SHARED, SHARED + HALF)
TILE = 256


def swap_cores(value):
    return lax.ppermute(value, "core", [(0, 1), (1, 0)])


def near(value, axis):
    pairs = [(2 * i + c, 2 * ((i + (1, 3)[c]) % 4) + c) for i in range(4) for c in range(2)]
    return lax.ppermute(value, (axis, "core"), pairs)


def far(value, axis):
    pairs = [(2 * i + c, 2 * ((i + 2) % 4) + c) for i in range(4) for c in range(2)]
    return lax.ppermute(value, (axis, "core"), pairs)


def block_products(m, blocks, chunks, head, logits, fresh):
    width = logits.shape[2]
    top = 0
    for count, piece in chunks:
        parts = [piece(m, j) for j in blocks]
        for start in range(0, width, TILE):
            end = min(start + TILE, width)
            product = sum(
                jnp.dot(part, head[j * 1280 : (j + 1) * 1280, start:end], preferred_element_type=jnp.float32)
                for j, part in zip(blocks, parts)
            )
            if fresh:
                logits[m, top : top + count, start:end] = product
            else:
                logits[m, top : top + count, start:end] += product
        top += count


def row_stats(logits, ids, packed):
    chunk = 64
    lane = lax.broadcasted_iota(jnp.int32, (chunk, 128), 1)
    tiles = range(0, logits.shape[2], 128)

    def finish(i, carry):
        here = pl.ds(pl.multiple_of(i * chunk, chunk), chunk)
        top_p = jnp.max(
            functools.reduce(jnp.maximum, [logits[0, here, t : t + 128] for t in tiles]), axis=-1, keepdims=True
        )
        top_q = jnp.max(
            functools.reduce(jnp.maximum, [logits[1, here, t : t + 128] for t in tiles]), axis=-1, keepdims=True
        )
        relative = None if ids is None else ids[here, :] - lane
        sums = None
        for t in tiles:
            p, q = logits[0, here, t : t + 128], logits[1, here, t : t + 128]
            expo = jnp.exp(p - top_p)
            terms = expo, expo * (p - q), jnp.exp(q - top_q)
            if ids is not None:
                terms += (jnp.where(relative == t, p, 0.0),)
            sums = terms if sums is None else tuple(a + b for a, b in zip(sums, terms))
        sum_p, cross, sum_q, *chosen = (jnp.sum(v, axis=-1, keepdims=True) for v in sums)
        found = jnp.where(lane == 0, top_p + jnp.log(sum_p), 0.0)
        found = jnp.where(lane == 1, cross / sum_p, found)
        found = jnp.where(lane == 2, top_q + jnp.log(sum_q), found)
        packed[here, :] = jnp.where(lane == 3, chosen[0], found) if chosen else found
        return carry

    lax.fori_loop(0, logits.shape[1] // chunk, finish, 0)


def near_blocks(where_ref):
    x = where_ref[2]
    return [lax.rem(x + d, 4) for d in (0, 3, 1, 2)]


def placed_blocks(places, where_ref):
    y, z, core = where_ref[0], where_ref[1], where_ref[3]
    blocks = []
    for kind, by_core in places:
        for (along_0, across_0), (along_1, across_1) in zip(*by_core):
            along = jnp.where(core == 0, along_0, along_1)
            across = jnp.where(core == 0, across_0, across_1)
            dy, dz = (along, across) if kind == 0 else (across, along)
            ctx = lax.rem(y + dy, 4) * 4 + lax.rem(z + dz, 4)
            blocks.append((ctx, STARTS[kind]))
    return blocks


def moved_chunks(refs):
    def chunk(some):
        return 2 * HALF * len(some), lambda m, j: jnp.concatenate([ref[m, j] for ref in some], axis=0)

    return [chunk(refs[i : i + 4]) for i in range(0, len(refs), 4)]


def take_ids(blocks, ids_ref, ids):
    for i, (ctx, start) in enumerate(blocks):
        ids[i * HALF : (i + 1) * HALF, :] = ids_ref[ctx, start : start + HALF, :]


def give_stats(blocks, found, out_ref):
    for i, (ctx, start) in enumerate(blocks):
        out_ref[ctx, :, start : start + HALF] = found[:, i * HALF : (i + 1) * HALF]


def chosen_logits(logits, ids, packed):
    chunk = 64
    lane = lax.broadcasted_iota(jnp.int32, (chunk, 128), 1)

    def pick(i, carry):
        here = pl.ds(pl.multiple_of(i * chunk, chunk), chunk)
        relative = ids[here, :] - lane
        total = sum(
            jnp.where(relative == t, logits[here, t : t + 128], 0.0) for t in range(0, logits.shape[1], 128)
        )
        packed[here, :] = jnp.where(lane == 3, jnp.sum(total, axis=-1, keepdims=True), 0.0)
        return carry

    lax.fori_loop(0, logits.shape[0] // chunk, pick, 0)


class HeadBlocks:
    ahead = 4

    def __init__(self, heads, near_to, buffer, sems):
        self.order = [(m, j) for m in range(2) for j in range(4)]
        self.copies = [
            pltpu.make_async_copy(
                heads[m].at[pl.ds(pl.multiple_of(near_to[j] * 1280, 1280), 1280)],
                buffer.at[m, pl.ds(j * 1280, 1280)],
                sems.at[m, j],
            )
            for m, j in self.order
        ]
        for copy in self.copies[: self.ahead]:
            copy.start()

    def wait(self, k):
        self.copies[k].wait()
        if k + self.ahead < len(self.copies):
            self.copies[k + self.ahead].start()


def early_kernel(places, where_ref, *refs):
    count = len(places)
    moved, heads = refs[:count], refs[count : count + 2]
    out_ref, logits_ref, packed, logits, buffer, sems = refs[count + 2 :]
    stream = HeadBlocks(heads, near_blocks(where_ref), buffer, sems)
    chunks = moved_chunks(moved)
    for i in range(0, 8, 2):
        m, j = stream.order[i]
        stream.wait(i)
        stream.wait(i + 1)
        block_products(m, (j, j + 1), chunks, buffer.at[m], logits, j == 0)
    row_stats(logits, None, packed)
    logits_ref[...] = logits[0]
    give_stats(placed_blocks(places, where_ref), packed[...].T[0:8], out_ref)


def late_kernel(places, earlier, where_ref, ids_ref, *refs):
    count = len(places)
    moved, source, heads, earlier_logits = refs[:count], refs[count], refs[count + 1 : count + 3], refs[count + 3]
    out_ref, packed, logits, buffer, sems, hidden, hidden_sems, ids = refs[-8:]
    near_to = near_blocks(where_ref)
    stream = HeadBlocks(heads, near_to, buffer, sems)
    shared = [
        pltpu.make_async_copy(source.at[:, near_to[j], :, pl.ds(0, 2 * SHARED)], hidden.at[j], hidden_sems.at[j])
        for j in range(4)
    ]
    for copy in shared:
        copy.start()
    before = placed_blocks(earlier, where_ref)
    take_ids(before, ids_ref, ids)
    chosen_logits(earlier_logits, ids, packed)
    found = packed[...].T[0:8]
    for i, (ctx, start) in enumerate(before):
        out_ref[ctx, 3:4, start : start + HALF] = found[3:4, i * HALF : (i + 1) * HALF]

    blocks = placed_blocks(places, where_ref)
    first, rows = HALF * len(blocks), 16 * SHARED
    take_ids(blocks, ids_ref, ids)
    ids[first : first + rows, :] = ids_ref[:, 0:SHARED, :].reshape(rows, 1)

    def piece(m, j):
        halves = [hidden[j, :, c, m * SHARED : (m + 1) * SHARED].reshape(rows, 640) for c in range(2)]
        return jnp.concatenate(halves, axis=1)

    chunks = moved_chunks(moved) + [(rows, piece)]
    for i in range(0, 8, 2):
        m, j = stream.order[i]
        for k in (i, i + 1):
            stream.wait(k)
            if m == 0:
                shared[k].wait()
        block_products(m, (j, j + 1), chunks, buffer.at[m], logits, j == 0)
    row_stats(logits, ids, packed)
    found = packed[...].T[0:8]
    give_stats(blocks, found, out_ref)
    for ctx in range(16):
        out_ref[ctx, :, 0:SHARED] = found[:, first + ctx * SHARED : first + (ctx + 1) * SHARED]


def stats_call(kernel, name, rows, operands, spaces, heads, outs, scratch, aliases):
    depth, width = heads[0].shape
    return pl.pallas_call(
        kernel,
        in_specs=[pl.BlockSpec(memory_space=space) for space in spaces],
        out_specs=[pl.BlockSpec(memory_space=pltpu.VMEM)] * len(outs),
        out_shape=outs,
        scratch_shapes=[
            pltpu.VMEM((rows, 128), jnp.float32),
            pltpu.VMEM((2, rows, width), jnp.float32),
            pltpu.VMEM((2, depth, width), jnp.bfloat16),
            pltpu.SemaphoreType.DMA((2, 4)),
        ]
        + scratch,
        input_output_aliases=aliases,
        compiler_params=pltpu.CompilerParams(vmem_limit_bytes=47 << 20),
        cost_estimate=pl.CostEstimate(flops=1, bytes_accessed=1, transcendentals=0),
        name=name,
    )(*operands)


def early_stats(where, pieces, heads):
    rows = 2 * HALF * len(pieces)
    return stats_call(
        functools.partial(early_kernel, tuple(p for _, p in pieces)),
        "early_stats",
        rows,
        (where, *[a for a, _ in pieces], *heads),
        [pltpu.SMEM] + [pltpu.VMEM] * len(pieces) + [pltpu.HBM] * 2,
        heads,
        [
            jax.ShapeDtypeStruct((16, 8, 128), jnp.float32),
            jax.ShapeDtypeStruct((rows, heads[0].shape[1]), jnp.float32),
        ],
        [],
        {},
    )


def late_stats(where, ids, pieces, gathered, heads, earlier, earlier_logits, stats):
    rows = 2 * HALF * len(pieces) + 16 * SHARED
    operands = (where, ids, *[a for a, _ in pieces], gathered, *heads, earlier_logits, stats)
    return stats_call(
        functools.partial(late_kernel, tuple(p for _, p in pieces), tuple(p for _, p in earlier)),
        "late_stats",
        rows,
        operands,
        [pltpu.SMEM] + [pltpu.VMEM] * (1 + len(pieces)) + [pltpu.HBM] * 3 + [pltpu.VMEM] * 2,
        heads,
        [jax.ShapeDtypeStruct(stats.shape, stats.dtype)],
        [
            pltpu.VMEM((4, 16, 2, 2 * SHARED, 640), jnp.bfloat16),
            pltpu.SemaphoreType.DMA((4,)),
            pltpu.VMEM((rows, 1), jnp.int32),
        ],
        {len(operands) - 1: 0},
    )[0]


def chain_products(coef):
    count = coef.shape[1]
    t = lax.broadcasted_iota(jnp.int32, (1, count, count), 1)
    u = lax.broadcasted_iota(jnp.int32, (1, count, count), 2)
    before = jnp.concatenate([jnp.ones_like(coef[:, :1]), coef[:, :-1]], axis=1)
    factors = jnp.where(u > t, before[:, None, :], 1.0)
    shift = 1
    while shift < count:
        moved = jnp.pad(factors[:, :, :-shift], ((0, 0), (0, 0), (shift, 0)), constant_values=1.0)
        factors = factors * moved
        shift *= 2
    return jnp.where(u >= t, factors, 0.0)


def split_exact(value):
    parts = []
    for _ in range(3):
        part = lax.reduce_precision(value, 8, 7)
        parts.append(part)
        value = value - part
    return parts


def gather_line(first, value, axis):
    beside, across = near(value, axis), far(jnp.where(first, value[0], value[1]), axis)
    beside_2, across_2 = swap_cores(beside), swap_cores(across)
    before = jnp.where(first, beside, beside_2)
    after = jnp.where(first, beside_2, beside)
    opposite = jnp.stack([jnp.where(first, across, across_2), jnp.where(first, across_2, across)])
    return value, before, after, opposite


def body(hidden_policy, hidden_ref, head_policy, head_ref, token_ids, response_mask, done_flags, scores, values):
    y, z, x, core = (lax.axis_index(a) for a in ALL)
    width = head_policy.shape[1]
    tok = token_ids.shape[1]
    ctx = y * 4 + z
    first = core == 0
    where = jnp.stack([y, z, x, core])
    heads = (head_policy, head_ref)

    both = jnp.stack([hidden_policy.reshape(64, 640), hidden_ref.reshape(64, 640)])
    rest = both[:, SHARED:]
    got = swap_cores(rest)
    rest = jnp.concatenate([jnp.where(first, rest, got), jnp.where(first, got, rest)], axis=-1)

    mask = response_mask.astype(jnp.float32)
    done = done_flags.astype(jnp.float32)
    coef = 0.998 * (1.0 - done)
    products = chain_products(coef)
    decay = products[:, :, -1] * coef[:, -1:]

    digits = [token_ids & 255, (token_ids >> 8) & 255, token_ids >> 16]
    numbers = split_exact(jnp.stack([decay[:, 0], values[:, 0]]))
    extra = jnp.concatenate(
        [d.reshape(64).astype(jnp.bfloat16) for d in digits] + [n.reshape(4).astype(jnp.bfloat16) for n in numbers]
    )
    extra = jnp.pad(extra[None], ((0, 7), (0, 640 - extra.shape[0])))
    gathered = lax.all_gather(jnp.concatenate([both[:, :SHARED].reshape(2 * SHARED, 640), extra]), ALL)
    gathered = gathered.reshape(16, 4, 2, 2 * SHARED + 8, 640)
    extra = gathered[:, 0, 0, 2 * SHARED, :256].astype(jnp.float32)
    ids = (extra[:, :64] + 256.0 * extra[:, 64:128] + 65536.0 * extra[:, 128:192]).astype(jnp.int32)
    ids = (ids - (ctx * 8 + x * 2 + core) * width)[:, :, None]
    numbers = extra[:, 192:196] + extra[:, 196:200] + extra[:, 200:204]
    head_decay, first_value = numbers[:, :2].T, numbers[:, 2:].T

    line = jnp.stack(gather_line(first, rest, "x"), axis=1)
    arrays = []
    for kind, (axis_2, axis_3) in enumerate((("z", "y"), ("y", "z"))):
        own, before, after, opposite = gather_line(first, line[:, :, kind * HALF : (kind + 1) * HALF], axis_2)
        lower = jnp.concatenate([own, before], axis=2)
        upper = jnp.concatenate([after, opposite], axis=2)
        arrays.append((jnp.where(first, lower, upper), jnp.where(first, upper, lower), axis_3))

    place = lax.broadcasted_iota(jnp.int32, (1, 16), 1)
    following = jnp.sum(jnp.where(place == ctx + 1, first_value, 0.0), axis=1, keepdims=True)
    next_value = jnp.concatenate([values[:, 1:], following], axis=1)
    known = done * scores + (1.0 - done) * next_value - values
    later = chain_products(head_decay)
    weights = jnp.sum(jnp.where(lax.broadcasted_iota(jnp.int32, (1, 16, 1), 1) == ctx + 1, later, 0.0), axis=1)

    def place_of(kind, along, halves):
        across = (0, 3, 1, 2)
        return kind, tuple(
            tuple((along[c], s) for s in across[2 * halves[c] : 2 * halves[c] + 2]) for c in range(2)
        )

    ones, twos, axes = zip(*arrays)
    kinds = range(2)
    ones_1 = [near(ones[k], axes[k]) for k in kinds]
    twos_1 = [near(twos[k], axes[k]) for k in kinds]
    ones_2 = [near(ones_1[k], axes[k]) for k in kinds]
    others_1 = [swap_cores(ones_1[k]) for k in kinds]
    early = [(ones[k], place_of(k, (0, 0), (0, 1))) for k in kinds]
    early += [(twos[k], place_of(k, (0, 0), (1, 0))) for k in kinds]
    early += [(ones_1[k], place_of(k, (3, 1), (0, 1))) for k in kinds]
    early += [(others_1[k], place_of(k, (1, 3), (1, 0))) for k in kinds]
    stats, early_logits = early_stats(where, early, heads)
    *arrived, stats = lax.optimization_barrier((*twos_1, *ones_2, stats))
    twos_1, ones_2 = arrived[:2], arrived[2:]
    late = [(twos_1[k], place_of(k, (3, 1), (1, 0))) for k in kinds]
    late += [(swap_cores(twos_1[k]), place_of(k, (1, 3), (0, 1))) for k in kinds]
    late += [(ones_2[k], place_of(k, (2, 2), (0, 1))) for k in kinds]
    late += [(swap_cores(ones_2[k]), place_of(k, (2, 2), (1, 0))) for k in kinds]
    stats = late_stats(where, ids, late, gathered, heads, early, early_logits, stats)

    stats = jnp.broadcast_to(stats[:, :4, :64].reshape(16, 1, 256), (16, 8, 256)).reshape(128, 256)
    stats = lax.all_to_all(stats, ALL, 0, 0, tiled=True).reshape(128, 4, 2, tok)
    lse_p, ratio, lse_q, chosen = (stats[:, i] for i in range(4))
    top_p = jnp.max(lse_p, axis=0)
    w_p = jnp.exp(lse_p - top_p)
    total = jnp.sum(w_p, axis=0)
    lz_p = top_p + jnp.log(total)
    top_q = jnp.max(lse_q, axis=0)
    lz_q = top_q + jnp.log(jnp.sum(jnp.exp(lse_q - top_q), axis=0))
    kl_val = jnp.sum(w_p * ratio, axis=0) / total - lz_p + lz_q
    logprobs = jnp.sum(chosen, axis=0) - lz_p
    penalty = -0.05 * mask * kl_val
    rewards = penalty + done * scores
    delta = penalty + known
    local_gae = jnp.sum(products * delta[:, None, :], axis=2)
    fronts = lax.all_to_all(jnp.broadcast_to(local_gae[:, 0][None], (16, 2)), PLANE, 0, 0, tiled=True)
    incoming = jnp.sum(weights * fronts.T, axis=1, keepdims=True)
    gae = local_gae + decay * incoming
    return rewards, mask * gae, mask * (gae + values), logprobs


def solution(mesh):
    fine = Mesh(np.asarray(mesh.devices).reshape(4, 4, 4, 2), ALL)
    placed = (P(None, PLANE, VOCAB),) * 2 + (P(None, ALL),) * 2 + (P(None, PLANE),) * 5
    return jax.shard_map(
        body,
        mesh=fine,
        in_specs=placed,
        out_specs=(P(None, PLANE),) * 4,
        check_vma=False,
    )
```

```python
import functools

import jax
import jax.numpy as jnp
import numpy as np
from jax import lax
from jax.experimental import pallas as pl
from jax.experimental.pallas import tpu as pltpu
from jax.sharding import Mesh, PartitionSpec as P


PLANE = ("y", "z")
VOCAB = ("x", "core")
ALL = PLANE + VOCAB
HALF = 32
STARTS = (0, HALF)
TILE = 256


def swap_cores(value):
    return lax.ppermute(value, "core", [(0, 1), (1, 0)])


def near(value, axis):
    pairs = [(2 * i + c, 2 * ((i + (1, 3)[c]) % 4) + c) for i in range(4) for c in range(2)]
    return lax.ppermute(value, (axis, "core"), pairs)


def far(value, axis):
    pairs = [(2 * i + c, 2 * ((i + 2) % 4) + c) for i in range(4) for c in range(2)]
    return lax.ppermute(value, (axis, "core"), pairs)


def block_products(m, blocks, chunks, head, logits, fresh):
    width = logits.shape[2]
    top = 0
    for count, piece in chunks:
        parts = [piece(m, j) for j in blocks]
        for start in range(0, width, TILE):
            end = min(start + TILE, width)
            product = sum(
                jnp.dot(part, head[j * 1280 : (j + 1) * 1280, start:end], preferred_element_type=jnp.float32)
                for j, part in zip(blocks, parts)
            )
            if fresh:
                logits[m, top : top + count, start:end] = product
            else:
                logits[m, top : top + count, start:end] += product
        top += count


def row_stats(logits, ids, packed):
    chunk = 64
    lane = lax.broadcasted_iota(jnp.int32, (chunk, 128), 1)
    tiles = range(0, logits.shape[2], 128)

    def finish(i, carry):
        here = pl.ds(pl.multiple_of(i * chunk, chunk), chunk)
        top_p = jnp.max(
            functools.reduce(jnp.maximum, [logits[0, here, t : t + 128] for t in tiles]), axis=-1, keepdims=True
        )
        top_q = jnp.max(
            functools.reduce(jnp.maximum, [logits[1, here, t : t + 128] for t in tiles]), axis=-1, keepdims=True
        )
        relative = ids[here, :] - lane
        sums = None
        for t in tiles:
            p, q = logits[0, here, t : t + 128], logits[1, here, t : t + 128]
            expo = jnp.exp(p - top_p)
            terms = expo, expo * (p - q), jnp.exp(q - top_q), jnp.where(relative == t, p, 0.0)
            sums = terms if sums is None else tuple(a + b for a, b in zip(sums, terms))
        sum_p, cross, sum_q, chosen = (jnp.sum(v, axis=-1, keepdims=True) for v in sums)
        found = jnp.where(lane == 0, top_p + jnp.log(sum_p), 0.0)
        found = jnp.where(lane == 1, cross / sum_p, found)
        found = jnp.where(lane == 2, top_q + jnp.log(sum_q), found)
        packed[here, :] = jnp.where(lane == 3, chosen, found)
        return carry

    lax.fori_loop(0, logits.shape[1] // chunk, finish, 0)


def near_blocks(where_ref):
    x = where_ref[2]
    return [lax.rem(x + d, 4) for d in (0, 3, 1, 2)]


def placed_blocks(places, where_ref):
    y, z, core = where_ref[0], where_ref[1], where_ref[3]
    blocks = []
    for kind, by_core in places:
        for (along_0, across_0), (along_1, across_1) in zip(*by_core):
            along = jnp.where(core == 0, along_0, along_1)
            across = jnp.where(core == 0, across_0, across_1)
            dy, dz = (along, across) if kind == 0 else (across, along)
            ctx = lax.rem(y + dy, 4) * 4 + lax.rem(z + dz, 4)
            blocks.append((ctx, STARTS[kind]))
    return blocks


def moved_chunks(refs):
    def chunk(some):
        return 2 * HALF * len(some), lambda m, j: jnp.concatenate([ref[m, j] for ref in some], axis=0)

    return [chunk(refs[i : i + 4]) for i in range(0, len(refs), 4)]


def take_ids(blocks, ids_ref, ids):
    for i, (ctx, start) in enumerate(blocks):
        ids[i * HALF : (i + 1) * HALF, :] = ids_ref[ctx, start : start + HALF, :]


def give_stats(blocks, found, out_ref):
    for i, (ctx, start) in enumerate(blocks):
        out_ref[ctx, :, start : start + HALF] = found[:, i * HALF : (i + 1) * HALF]


class HeadBlocks:
    ahead = 4

    def __init__(self, heads, near_to, buffer, sems):
        self.order = [(m, j) for m in range(2) for j in range(4)]
        self.copies = [
            pltpu.make_async_copy(
                heads[m].at[pl.ds(pl.multiple_of(near_to[j] * 1280, 1280), 1280)],
                buffer[m].at[pl.ds(j * 1280, 1280)] if isinstance(buffer, tuple) else buffer.at[m, pl.ds(j * 1280, 1280)],
                sems.at[m, j],
            )
            for m, j in self.order
        ]
        for copy in self.copies[: self.ahead]:
            copy.start()

    def wait(self, k):
        self.copies[k].wait()
        if k + self.ahead < len(self.copies):
            self.copies[k + self.ahead].start()


def early_kernel(places, where_ref, ids_ref, *refs):
    count = len(places)
    sources, heads = refs[:count], refs[count : count + 2]
    out_ref, packed, logits, ids, sems, buffer, moved, moved_sems = refs[count + 2 :]
    inputs = [
        [pltpu.make_async_copy(sources[k].at[m], moved.at[k, m], moved_sems.at[k, m]) for k in range(count)]
        for m in range(2)
    ]
    for copy in inputs[0]:
        copy.start()
    stream = HeadBlocks(heads, near_blocks(where_ref), buffer, sems)
    for copy in inputs[1]:
        copy.start()
    blocks = placed_blocks(places, where_ref)
    take_ids(blocks, ids_ref, ids)
    chunks = moved_chunks([moved.at[k] for k in range(count)])
    for m, groups in enumerate((((0,), (1,), (2, 3)), ((0, 1), (2, 3)))):
        for copy in inputs[m]:
            copy.wait()
        for group in groups:
            for j in group:
                stream.wait(4 * m + j)
            block_products(m, group, chunks, buffer.at[m], logits, group[0] == 0)
    row_stats(logits, ids, packed)
    give_stats(blocks, packed[...].T[0:8], out_ref)


def late_kernel(places, where_ref, ids_ref, *refs):
    count = len(places)
    moved, heads = refs[:count], refs[count : count + 2]
    out_ref, head_p, head_q, packed, logits, ids, sems = refs[count + 3 :]
    buffer = (head_p, head_q)
    stream = HeadBlocks(heads, near_blocks(where_ref), buffer, sems)
    blocks = placed_blocks(places, where_ref)
    take_ids(blocks, ids_ref, ids)
    chunks = moved_chunks(moved)
    for m, groups in enumerate((((0,), (1,), (2, 3)), ((0, 1), (2,), (3,)))):
        for group in groups:
            for j in group:
                stream.wait(4 * m + j)
            block_products(m, group, chunks, buffer[m], logits, group[0] == 0)
    row_stats(logits, ids, packed)
    give_stats(blocks, packed[...].T[0:8], out_ref)


def last_kernel(places, where_ref, ids_ref, *refs):
    count = len(places)
    moved, heads = refs[:count], refs[count : count + 2]
    out_ref, packed, logits, ids, sems = refs[count + 3 :]
    blocks = placed_blocks(places, where_ref)
    take_ids(blocks, ids_ref, ids)
    chunks = moved_chunks(moved)
    for m in range(2):
        block_products(m, range(4), chunks, heads[m], logits, True)
    row_stats(logits, ids, packed)
    give_stats(blocks, packed[...].T[0:8], out_ref)


def stats_call(kernel, name, where, ids, pieces, heads, before, limit):
    vmem, hbm = pl.BlockSpec(memory_space=pltpu.VMEM), pl.BlockSpec(memory_space=pltpu.HBM)
    depth, width = heads[0].shape
    count = len(pieces)
    rows = 2 * HALF * count
    chain = () if before is None else (before,)
    operands = (where, ids, *[a for a, _ in pieces], *heads, *chain)
    early, late = kernel is early_kernel, kernel is late_kernel
    outs = [jax.ShapeDtypeStruct((16, 8, 128), jnp.float32)]
    if late:
        outs += [jax.ShapeDtypeStruct(h.shape, h.dtype) for h in heads]
    scratch = [
        pltpu.VMEM((rows, 128), jnp.float32),
        pltpu.VMEM((2, rows, width), jnp.float32),
        pltpu.VMEM((rows, 1), jnp.int32),
        pltpu.SemaphoreType.DMA((2, 4)),
    ]
    if early:
        scratch += [
            pltpu.VMEM((2, depth, width), jnp.bfloat16),
            pltpu.VMEM((count, 2, 4, 2 * HALF, 1280), jnp.bfloat16),
            pltpu.SemaphoreType.DMA((count, 2)),
        ]
    return pl.pallas_call(
        functools.partial(kernel, tuple(p for _, p in pieces)),
        in_specs=[pl.BlockSpec(memory_space=pltpu.SMEM), vmem]
        + [hbm if early else vmem] * count
        + [hbm if early or late else vmem] * 2
        + [vmem] * len(chain),
        out_specs=[vmem] * len(outs),
        out_shape=outs,
        scratch_shapes=scratch,
        input_output_aliases={len(operands) - 1: 0} if chain else {},
        compiler_params=pltpu.CompilerParams(vmem_limit_bytes=limit << 20),
        cost_estimate=pl.CostEstimate(
            flops=4 * rows * depth * width,
            bytes_accessed=4 * depth * (rows + width),
            transcendentals=2 * rows * width,
        ),
        name=name,
    )(*operands)


def chain_products(coef):
    count = coef.shape[1]
    t = lax.broadcasted_iota(jnp.int32, (1, count, count), 1)
    u = lax.broadcasted_iota(jnp.int32, (1, count, count), 2)
    before = jnp.concatenate([jnp.ones_like(coef[:, :1]), coef[:, :-1]], axis=1)
    factors = jnp.where(u > t, before[:, None, :], 1.0)
    shift = 1
    while shift < count:
        moved = jnp.pad(factors[:, :, :-shift], ((0, 0), (0, 0), (shift, 0)), constant_values=1.0)
        factors = factors * moved
        shift *= 2
    return jnp.where(u >= t, factors, 0.0)


def gather_line(first, value, axis):
    beside, across = near(value, axis), far(jnp.where(first, value[0], value[1]), axis)
    beside_2, across_2 = swap_cores(beside), swap_cores(across)
    before = jnp.where(first, beside, beside_2)
    after = jnp.where(first, beside_2, beside)
    opposite = jnp.stack([jnp.where(first, across, across_2), jnp.where(first, across_2, across)])
    return value, before, after, opposite


def body(hidden_policy, hidden_ref, head_policy, head_ref, token_ids, response_mask, done_flags, scores, values):
    y, z, x, core = (lax.axis_index(a) for a in ALL)
    width = head_policy.shape[1]
    tok = token_ids.shape[1]
    ctx = y * 4 + z
    first = core == 0
    where = jnp.stack([y, z, x, core])
    heads = (head_policy, head_ref)

    both = jnp.stack([hidden_policy.reshape(64, 640), hidden_ref.reshape(64, 640)])
    got = swap_cores(both)
    rest = jnp.concatenate([jnp.where(first, both, got), jnp.where(first, got, both)], axis=-1)

    mask = response_mask.astype(jnp.float32)
    done = done_flags.astype(jnp.float32)
    coef = 0.998 * (1.0 - done)
    products = chain_products(coef)
    decay = products[:, :, -1] * coef[:, -1:]

    line = jnp.stack(gather_line(first, rest, "x"), axis=1)
    shared = jnp.concatenate(
        [token_ids.astype(jnp.float32), decay[:, :1], values[:, :1], jnp.zeros((2, 30), jnp.float32)], axis=1
    )
    shared, line = lax.optimization_barrier((shared, line))
    shared = lax.all_to_all(jnp.broadcast_to(shared.reshape(1, 128), (16, 128)), PLANE, 0, 0, tiled=True)
    shared = shared.reshape(16, 2, 64)
    columns = (ctx * 8 + x * 2 + core) * width
    ids = shared[:, :, :tok].reshape(16, 64, 1).astype(jnp.int32) - columns
    head_decay, first_value = shared[:, :, tok].T, shared[:, :, tok + 1].T

    arrays = []
    for kind, (axis_2, axis_3) in enumerate((("z", "y"), ("y", "z"))):
        own, before, after, opposite = gather_line(first, line[:, :, kind * HALF : (kind + 1) * HALF], axis_2)
        own, before, after, opposite, ids = lax.optimization_barrier((own, before, after, opposite, ids))
        lower = jnp.concatenate([own, before], axis=2)
        upper = jnp.concatenate([after, opposite], axis=2)
        arrays.append((jnp.where(first, lower, upper), jnp.where(first, upper, lower), axis_3))

    place = lax.broadcasted_iota(jnp.int32, (1, 16), 1)
    following = jnp.sum(jnp.where(place == ctx + 1, first_value, 0.0), axis=1, keepdims=True)
    next_value = jnp.concatenate([values[:, 1:], following], axis=1)
    known = done * scores + (1.0 - done) * next_value - values
    later = chain_products(head_decay)
    weights = jnp.sum(jnp.where(lax.broadcasted_iota(jnp.int32, (1, 16, 1), 1) == ctx + 1, later, 0.0), axis=1)

    def place_of(kind, along, halves):
        across = (0, 3, 1, 2)
        return kind, tuple(
            tuple((along[c], s) for s in across[2 * halves[c] : 2 * halves[c] + 2]) for c in range(2)
        )

    ones, twos, axes = zip(*arrays)
    kinds = range(2)
    ones_1 = [near(ones[k], axes[k]) for k in kinds]
    twos_1 = [near(twos[k], axes[k]) for k in kinds]
    ones_2 = [near(ones_1[k], axes[k]) for k in kinds]
    others_1 = [swap_cores(ones_1[k]) for k in kinds]
    early = [(ones[k], place_of(k, (0, 0), (0, 1))) for k in kinds]
    early += [(twos[k], place_of(k, (0, 0), (1, 0))) for k in kinds]
    early += [(ones_1[k], place_of(k, (3, 1), (0, 1))) for k in kinds]
    early += [(others_1[k], place_of(k, (1, 3), (1, 0))) for k in kinds]
    (stats,) = stats_call(early_kernel, "early_stats", where, ids, early, heads, None, 54)
    *arrived, stats = lax.optimization_barrier((*twos_1, *ones_2, stats))
    twos_1, ones_2 = arrived[:2], arrived[2:]
    late = [(twos_1[k], place_of(k, (3, 1), (1, 0))) for k in kinds]
    late += [(ones_2[k], place_of(k, (2, 2), (0, 1))) for k in kinds]
    last = [(swap_cores(twos_1[k]), place_of(k, (1, 3), (0, 1))) for k in kinds]
    last += [(swap_cores(ones_2[k]), place_of(k, (2, 2), (1, 0))) for k in kinds]
    stats, *heads = stats_call(late_kernel, "late_stats", where, ids, late, heads, stats, 24)
    (stats,) = stats_call(last_kernel, "last_stats", where, ids, last, heads, stats, 24)

    stats = jnp.broadcast_to(stats[:, :4, :64].reshape(16, 1, 256), (16, 8, 256)).reshape(128, 256)
    stats = lax.all_to_all(stats, ALL, 0, 0, tiled=True).reshape(128, 4, 2, tok)
    lse_p, ratio, lse_q, chosen = (stats[:, i] for i in range(4))
    top_p = jnp.max(lse_p, axis=0)
    w_p = jnp.exp(lse_p - top_p)
    total = jnp.sum(w_p, axis=0)
    lz_p = top_p + jnp.log(total)
    top_q = jnp.max(lse_q, axis=0)
    lz_q = top_q + jnp.log(jnp.sum(jnp.exp(lse_q - top_q), axis=0))
    kl_val = jnp.sum(w_p * ratio, axis=0) / total - lz_p + lz_q
    logprobs = jnp.sum(chosen, axis=0) - lz_p
    penalty = -0.05 * mask * kl_val
    rewards = penalty + done * scores
    delta = penalty + known
    local_gae = jnp.sum(products * delta[:, None, :], axis=2)
    fronts = lax.all_to_all(jnp.broadcast_to(local_gae[:, 0][None], (16, 2)), PLANE, 0, 0, tiled=True)
    incoming = jnp.sum(weights * fronts.T, axis=1, keepdims=True)
    gae = local_gae + decay * incoming
    return rewards, mask * gae, mask * (gae + values), logprobs


def solution(mesh):
    fine = Mesh(np.asarray(mesh.devices).reshape(4, 4, 4, 2), ALL)
    placed = (P(None, PLANE, VOCAB),) * 2 + (P(None, ALL),) * 2 + (P(None, PLANE),) * 5
    return jax.shard_map(
        body,
        mesh=fine,
        in_specs=placed,
        out_specs=(P(None, PLANE),) * 4,
        check_vma=False,
    )
```

```python
import functools

import jax
import jax.numpy as jnp
import numpy as np
from jax import lax
from jax.experimental import pallas as pl
from jax.experimental.pallas import tpu as pltpu
from jax.sharding import Mesh, PartitionSpec as P


PLANE = ("y", "z")
VOCAB = ("x", "core")
ALL = PLANE + VOCAB
HALF = 32
STARTS = (0, HALF)
TILE = 256


def swap_cores(value):
    return lax.ppermute(value, "core", [(0, 1), (1, 0)])


def near(value, axis):
    pairs = [(2 * i + c, 2 * ((i + (1, 3)[c]) % 4) + c) for i in range(4) for c in range(2)]
    return lax.ppermute(value, (axis, "core"), pairs)


def far(value, axis):
    pairs = [(2 * i + c, 2 * ((i + 2) % 4) + c) for i in range(4) for c in range(2)]
    return lax.ppermute(value, (axis, "core"), pairs)


def block_products(m, blocks, chunks, head, logits, fresh):
    width = logits.shape[2]
    top = 0
    for count, piece in chunks:
        parts = [piece(m, j) for j in blocks]
        for start in range(0, width, TILE):
            end = min(start + TILE, width)
            product = sum(
                jnp.dot(part, head[j * 1280 : (j + 1) * 1280, start:end], preferred_element_type=jnp.float32)
                for j, part in zip(blocks, parts)
            )
            if fresh:
                logits[m, top : top + count, start:end] = product
            else:
                logits[m, top : top + count, start:end] += product
        top += count


def row_stats(logits, ids, packed):
    chunk = 256
    lane = lax.broadcasted_iota(jnp.int32, (chunk, 128), 1)
    tiles = range(0, logits.shape[2], 128)

    def finish(i, carry):
        here = pl.ds(pl.multiple_of(i * chunk, chunk), chunk)
        top_p = jnp.max(
            functools.reduce(jnp.maximum, [logits[0, here, t : t + 128] for t in tiles]), axis=-1, keepdims=True
        )
        top_q = jnp.max(
            functools.reduce(jnp.maximum, [logits[1, here, t : t + 128] for t in tiles]), axis=-1, keepdims=True
        )
        relative = ids[here, :] - lane
        sums = None
        for t in tiles:
            p, q = logits[0, here, t : t + 128], logits[1, here, t : t + 128]
            expo = jnp.exp(p - top_p)
            terms = expo, expo * (p - q), jnp.exp(q - top_q), jnp.where(relative == t, p, 0.0)
            sums = terms if sums is None else tuple(a + b for a, b in zip(sums, terms))
        sum_p, cross, sum_q, chosen = (jnp.sum(v, axis=-1, keepdims=True) for v in sums)
        found = jnp.where(lane == 0, top_p + jnp.log(sum_p), 0.0)
        found = jnp.where(lane == 1, cross / sum_p, found)
        found = jnp.where(lane == 2, top_q + jnp.log(sum_q), found)
        packed[here, :] = jnp.where(lane == 3, chosen, found)
        return carry

    lax.fori_loop(0, logits.shape[1] // chunk, finish, 0)


def near_blocks(where_ref):
    x = where_ref[2]
    return [lax.rem(x + d, 4) for d in (0, 3, 1, 2)]


def placed_blocks(places, where_ref):
    y, z, core = where_ref[0], where_ref[1], where_ref[3]
    blocks = []
    for kind, by_core in places:
        for (along_0, across_0), (along_1, across_1) in zip(*by_core):
            along = jnp.where(core == 0, along_0, along_1)
            across = jnp.where(core == 0, across_0, across_1)
            dy, dz = (along, across) if kind == 0 else (across, along)
            ctx = lax.rem(y + dy, 4) * 4 + lax.rem(z + dz, 4)
            blocks.append((ctx, STARTS[kind]))
    return blocks


def moved_chunks(refs):
    def chunk(some):
        return 2 * HALF * len(some), lambda m, j: jnp.concatenate([ref[m, j] for ref in some], axis=0)

    return [chunk(refs[i : i + 4]) for i in range(0, len(refs), 4)]


def take_ids(blocks, ids_ref, ids):
    for i, (ctx, start) in enumerate(blocks):
        ids[i * HALF : (i + 1) * HALF, :] = ids_ref[ctx, start : start + HALF, :]


def give_stats(blocks, found, out_ref):
    for i, (ctx, start) in enumerate(blocks):
        out_ref[ctx, :, start : start + HALF] = found[:, i * HALF : (i + 1) * HALF]


class HeadBlocks:
    ahead = 6

    def __init__(self, heads, near_to, buffer, sems):
        self.order = [(m, j) for m in range(2) for j in range(4)]
        self.copies = [
            pltpu.make_async_copy(
                heads[m].at[pl.ds(pl.multiple_of(near_to[j] * 1280, 1280), 1280)],
                buffer[m].at[pl.ds(j * 1280, 1280)] if isinstance(buffer, tuple) else buffer.at[m, pl.ds(j * 1280, 1280)],
                sems.at[m, j],
            )
            for m, j in self.order
        ]
        for copy in self.copies[: self.ahead]:
            copy.start()

    def wait(self, k):
        self.copies[k].wait()
        if k + self.ahead < len(self.copies):
            self.copies[k + self.ahead].start()


def early_kernel(places, where_ref, ids_ref, *refs):
    count = len(places)
    sources, heads = refs[:count], refs[count : count + 2]
    out_ref, packed, logits, ids, sems, buffer, moved, moved_sems = refs[count + 2 :]
    inputs = [
        [pltpu.make_async_copy(sources[k].at[m], moved.at[k, m], moved_sems.at[k, m]) for k in range(count)]
        for m in range(2)
    ]
    for copy in inputs[0]:
        copy.start()
    stream = HeadBlocks(heads, near_blocks(where_ref), buffer, sems)
    for copy in inputs[1]:
        copy.start()
    blocks = placed_blocks(places, where_ref)
    take_ids(blocks, ids_ref, ids)
    chunks = moved_chunks([moved.at[k] for k in range(count)])
    for m, groups in enumerate((((0,), (1,), (2, 3)), ((0, 1), (2, 3)))):
        for copy in inputs[m]:
            copy.wait()
        for group in groups:
            for j in group:
                stream.wait(4 * m + j)
            block_products(m, group, chunks, buffer.at[m], logits, group[0] == 0)
    row_stats(logits, ids, packed)
    give_stats(blocks, packed[...].T[0:8], out_ref)


def late_kernel(places, where_ref, ids_ref, *refs):
    count = len(places)
    moved, heads = refs[:count], refs[count : count + 2]
    out_ref, head_p, head_q, packed, logits, ids, sems = refs[count + 3 :]
    buffer = (head_p, head_q)
    stream = HeadBlocks(heads, near_blocks(where_ref), buffer, sems)
    blocks = placed_blocks(places, where_ref)
    take_ids(blocks, ids_ref, ids)
    chunks = moved_chunks(moved)
    for m, groups in enumerate((((0,), (1,), (2, 3)), ((0, 1), (2,), (3,)))):
        for group in groups:
            for j in group:
                stream.wait(4 * m + j)
            block_products(m, group, chunks, buffer[m], logits, group[0] == 0)
    row_stats(logits, ids, packed)
    give_stats(blocks, packed[...].T[0:8], out_ref)


def last_kernel(places, where_ref, ids_ref, *refs):
    count = len(places)
    moved, heads = refs[:count], refs[count : count + 2]
    out_ref, packed, logits, ids, sems = refs[count + 3 :]
    blocks = placed_blocks(places, where_ref)
    take_ids(blocks, ids_ref, ids)
    chunks = moved_chunks(moved)
    for m in range(2):
        block_products(m, range(4), chunks, heads[m], logits, True)
    row_stats(logits, ids, packed)
    give_stats(blocks, packed[...].T[0:8], out_ref)


def stats_call(kernel, name, where, ids, pieces, heads, before, limit):
    vmem, hbm = pl.BlockSpec(memory_space=pltpu.VMEM), pl.BlockSpec(memory_space=pltpu.HBM)
    depth, width = heads[0].shape
    count = len(pieces)
    rows = 2 * HALF * count
    chain = () if before is None else (before,)
    operands = (where, ids, *[a for a, _ in pieces], *heads, *chain)
    early, late = kernel is early_kernel, kernel is late_kernel
    outs = [jax.ShapeDtypeStruct((16, 8, 128), jnp.float32)]
    if late:
        outs += [jax.ShapeDtypeStruct(h.shape, h.dtype) for h in heads]
    scratch = [
        pltpu.VMEM((rows, 128), jnp.float32),
        pltpu.VMEM((2, rows, width), jnp.float32),
        pltpu.VMEM((rows, 1), jnp.int32),
        pltpu.SemaphoreType.DMA((2, 4)),
    ]
    if early:
        scratch += [
            pltpu.VMEM((2, depth, width), jnp.bfloat16),
            pltpu.VMEM((count, 2, 4, 2 * HALF, 1280), jnp.bfloat16),
            pltpu.SemaphoreType.DMA((count, 2)),
        ]
    return pl.pallas_call(
        functools.partial(kernel, tuple(p for _, p in pieces)),
        in_specs=[pl.BlockSpec(memory_space=pltpu.SMEM), vmem]
        + [hbm if early else vmem] * count
        + [hbm if early or late else vmem] * 2
        + [vmem] * len(chain),
        out_specs=[vmem] * len(outs),
        out_shape=outs,
        scratch_shapes=scratch,
        input_output_aliases={len(operands) - 1: 0} if chain else {},
        compiler_params=pltpu.CompilerParams(vmem_limit_bytes=limit << 20),
        cost_estimate=pl.CostEstimate(
            flops=4 * rows * depth * width,
            bytes_accessed=4 * depth * (rows + width),
            transcendentals=2 * rows * width,
        ),
        name=name,
    )(*operands)


def chain_products(coef):
    count = coef.shape[1]
    t = lax.broadcasted_iota(jnp.int32, (1, count, count), 1)
    u = lax.broadcasted_iota(jnp.int32, (1, count, count), 2)
    before = jnp.concatenate([jnp.ones_like(coef[:, :1]), coef[:, :-1]], axis=1)
    factors = jnp.where(u > t, before[:, None, :], 1.0)
    shift = 1
    while shift < count:
        moved = jnp.pad(factors[:, :, :-shift], ((0, 0), (0, 0), (shift, 0)), constant_values=1.0)
        factors = factors * moved
        shift *= 2
    return jnp.where(u >= t, factors, 0.0)


def gather_line(first, value, axis):
    beside, across = near(value, axis), far(jnp.where(first, value[0], value[1]), axis)
    beside_2, across_2 = swap_cores(beside), swap_cores(across)
    before = jnp.where(first, beside, beside_2)
    after = jnp.where(first, beside_2, beside)
    opposite = jnp.stack([jnp.where(first, across, across_2), jnp.where(first, across_2, across)])
    return value, before, after, opposite


def body(hidden_policy, hidden_ref, head_policy, head_ref, token_ids, response_mask, done_flags, scores, values):
    y, z, x, core = (lax.axis_index(a) for a in ALL)
    width = head_policy.shape[1]
    tok = token_ids.shape[1]
    ctx = y * 4 + z
    first = core == 0
    where = jnp.stack([y, z, x, core])
    heads = (head_policy, head_ref)

    both = jnp.stack([hidden_policy.reshape(64, 640), hidden_ref.reshape(64, 640)])
    got = swap_cores(both)
    got, done_flags = lax.optimization_barrier((got, done_flags))
    rest = jnp.concatenate([jnp.where(first, both, got), jnp.where(first, got, both)], axis=-1)

    mask = response_mask.astype(jnp.float32)
    done = done_flags.astype(jnp.float32)
    coef = 0.998 * (1.0 - done)
    products = chain_products(coef)
    decay = products[:, :, -1] * coef[:, -1:]

    line = jnp.stack(gather_line(first, rest, "x"), axis=1)
    shared = jnp.concatenate(
        [token_ids.astype(jnp.float32), decay[:, :1], values[:, :1], jnp.zeros((2, 30), jnp.float32)], axis=1
    )
    shared, line = lax.optimization_barrier((shared, line))
    shared = lax.all_to_all(jnp.broadcast_to(shared.reshape(1, 128), (16, 128)), PLANE, 0, 0, tiled=True)
    shared = shared.reshape(16, 2, 64)
    columns = (ctx * 8 + x * 2 + core) * width
    ids = shared[:, :, :tok].reshape(16, 64, 1).astype(jnp.int32) - columns
    head_decay, first_value = shared[:, :, tok].T, shared[:, :, tok + 1].T

    arrays = []
    for kind, (axis_2, axis_3) in enumerate((("z", "y"), ("y", "z"))):
        own, before, after, opposite = gather_line(first, line[:, :, kind * HALF : (kind + 1) * HALF], axis_2)
        own, before, after, opposite, ids = lax.optimization_barrier((own, before, after, opposite, ids))
        lower = jnp.concatenate([own, before], axis=2)
        upper = jnp.concatenate([after, opposite], axis=2)
        arrays.append((jnp.where(first, lower, upper), jnp.where(first, upper, lower), axis_3))

    place = lax.broadcasted_iota(jnp.int32, (1, 16), 1)
    following = jnp.sum(jnp.where(place == ctx + 1, first_value, 0.0), axis=1, keepdims=True)
    next_value = jnp.concatenate([values[:, 1:], following], axis=1)
    known = done * scores + (1.0 - done) * next_value - values
    later = chain_products(head_decay)
    weights = jnp.sum(jnp.where(lax.broadcasted_iota(jnp.int32, (1, 16, 1), 1) == ctx + 1, later, 0.0), axis=1)

    def place_of(kind, along, halves):
        across = (0, 3, 1, 2)
        return kind, tuple(
            tuple((along[c], s) for s in across[2 * halves[c] : 2 * halves[c] + 2]) for c in range(2)
        )

    ones, twos, axes = zip(*arrays)
    kinds = range(2)
    ones_1 = [near(ones[k], axes[k]) for k in kinds]
    twos_1 = [near(twos[k], axes[k]) for k in kinds]
    ones_2 = [near(ones_1[k], axes[k]) for k in kinds]
    others_1 = [swap_cores(ones_1[k]) for k in kinds]
    early = [(ones[k], place_of(k, (0, 0), (0, 1))) for k in kinds]
    early += [(twos[k], place_of(k, (0, 0), (1, 0))) for k in kinds]
    early += [(ones_1[k], place_of(k, (3, 1), (0, 1))) for k in kinds]
    early += [(others_1[k], place_of(k, (1, 3), (1, 0))) for k in kinds]
    (stats,) = stats_call(early_kernel, "early_stats", where, ids, early, heads, None, 54)
    *arrived, stats = lax.optimization_barrier((*twos_1, *ones_2, stats))
    twos_1, ones_2 = arrived[:2], arrived[2:]
    late = [(twos_1[k], place_of(k, (3, 1), (1, 0))) for k in kinds]
    late += [(ones_2[k], place_of(k, (2, 2), (0, 1))) for k in kinds]
    last = [(swap_cores(twos_1[k]), place_of(k, (1, 3), (0, 1))) for k in kinds]
    last += [(swap_cores(ones_2[k]), place_of(k, (2, 2), (1, 0))) for k in kinds]
    stats, *heads = stats_call(late_kernel, "late_stats", where, ids, late, heads, stats, 24)
    (stats,) = stats_call(last_kernel, "last_stats", where, ids, last, heads, stats, 24)

    stats = jnp.broadcast_to(stats[:, :4, :64].reshape(16, 1, 256), (16, 8, 256)).reshape(128, 256)
    stats = lax.all_to_all(stats, ALL, 0, 0, tiled=True).reshape(128, 4, 2, tok)
    lse_p, ratio, lse_q, chosen = (stats[:, i] for i in range(4))
    top_p = jnp.max(lse_p, axis=0)
    w_p = jnp.exp(lse_p - top_p)
    total = jnp.sum(w_p, axis=0)
    lz_p = top_p + jnp.log(total)
    top_q = jnp.max(lse_q, axis=0)
    lz_q = top_q + jnp.log(jnp.sum(jnp.exp(lse_q - top_q), axis=0))
    kl_val = jnp.sum(w_p * ratio, axis=0) / total - lz_p + lz_q
    logprobs = jnp.sum(chosen, axis=0) - lz_p
    penalty = -0.05 * mask * kl_val
    rewards = penalty + done * scores
    delta = penalty + known
    local_gae = jnp.sum(products * delta[:, None, :], axis=2)
    fronts = lax.all_to_all(jnp.broadcast_to(local_gae[:, 0][None], (16, 2)), PLANE, 0, 0, tiled=True)
    incoming = jnp.sum(weights * fronts.T, axis=1, keepdims=True)
    gae = local_gae + decay * incoming
    return rewards, mask * gae, mask * (gae + values), logprobs


def solution(mesh):
    fine = Mesh(np.asarray(mesh.devices).reshape(4, 4, 4, 2), ALL)
    placed = (P(None, PLANE, VOCAB),) * 2 + (P(None, ALL),) * 2 + (P(None, PLANE),) * 5
    return jax.shard_map(
        body,
        mesh=fine,
        in_specs=placed,
        out_specs=(P(None, PLANE),) * 4,
        check_vma=False,
    )
```
